32 devices in a mesh: groups: 2 (over x), band: 2 (over core), gz: 8 (over z, y).
Axes of the slice: x: 2, y: 2, z: 4, core: 2. Of those that a mesh axis runs over, the one named last changes fastest.
Arguments:
- orbitals: bfloat16 [24, 64, 256, 256], P(('groups', 'band'), 'gz'), parts along dimension 0, may hold values from -3 to 3
- band_group: int32 [24], P(('groups', 'band')), parts along dimension 0, may hold values from 0 to 7
- occ_table: int32 [8], replicated, may hold values from 0 to 2048
- core_density: float32 [128, 256, 256], P(('groups', 'gz')), parts along dimension 0, may hold values from 0.1 to 12
Outputs:
- potential: float32 [128, 256, 256], P(('groups', 'gz')), parts along dimension 0
- residual: float32 [128, 256, 256], P(('groups', 'gz'), 'band'), parts along dimension 0
The draws below stay inside these ranges and needn't reach their ends.
There are 2 independent parts, one for each index of `groups`. The reference program is written for one: setup_inputs(seed, part) draws one part's arguments, and reference() takes and returns one part's arrays. A program takes and returns all parts, laid end to end along the dimension named above; an argument that names none is the same for every part. Nothing has to cross between parts.
All inputs are finite; a program needn't handle non-finite values.
Results may differ from the reference program's by a relative error of at most 0.0003.
Values sent between devices are 32-bit elements; how exact they have to be, the bound alone decides.
A program may use at most 64 MiB of HBM per device.

```python
import math
import jax
import jax.numpy as jnp
from jax import lax

NY = 256
NX = 256
NOCC = 8
ITERS = 3
BANDS = 12
NZ = 64


def draw_core_density(key, part):
    key = jax.random.fold_in(key, 11)
    first = jax.random.fold_in(key, 0)
    shape = (NZ, NY, NX)
    rising = 1.0 + 3.0 * jnp.arange(NZ, dtype=jnp.float32) / max(NZ - 1, 1)
    base = jnp.exp(jax.random.uniform(first, shape, jnp.float32, math.log(0.1), math.log(2.0)))
    return base * rising[:, None, None]


def touch_ends(array, own_key, least, high):
    longest = array.shape.index(max(array.shape))
    spots = []
    for shift in (0, 1):
        where = [jax.random.randint(jax.random.fold_in(own_key, axis), (), 0, length) for axis, length in enumerate(array.shape)]
        where[longest] = (where[longest] + shift) % array.shape[longest]
        spots.append(tuple(where))
    return array.at[spots[0]].set(least).at[spots[1]].set(high)


def steps_of(own_key, extent, cuts, least, largest):
    def one(position, blocks):
        heights = jax.random.uniform(jax.random.fold_in(jax.random.fold_in(own_key, 6), position), (blocks,), jnp.float32, least / len(cuts), largest / len(cuts))
        return jnp.repeat(jnp.exp(heights), extent[position] // blocks).reshape((-1,) + (1,) * (len(extent) - position - 1))

    gain = one(*cuts[0])
    for cut in cuts[1:]:
        gain = gain * one(*cut)
    return gain


def normal_values(key, extent, scale, most, shards=(), kind=jnp.bfloat16):
    level = steps_of(key, extent, shards, -0.22, 0.18) if shards else 1.0
    drawn = jax.random.normal(key, extent, jnp.float32) * scale * level
    return jnp.minimum(jnp.maximum(drawn, -most), most).astype(kind)


def setup_inputs(seed: int = 0, part: int = 0) -> dict:
    seeds = jax.random.split(jax.random.key(seed), 5)
    own_keys = jax.random.split(jax.random.fold_in(seeds[4], part), 5)
    orbitals = normal_values(own_keys[0], (BANDS, NZ, NY, NX), 0.5, 3.0, ((0, 2), (1, 8)))
    band_group = touch_ends(jax.random.randint(own_keys[1], (BANDS,), 0, NOCC), jax.random.fold_in(own_keys[1], 1), 0, NOCC - 1).astype(jnp.int32)
    occ_table = touch_ends(jax.random.randint(seeds[2], (NOCC,), 0, 2049), jax.random.fold_in(seeds[2], 1), 0, 2048).astype(jnp.int32)
    core_density = draw_core_density(jax.random.fold_in(jax.random.fold_in(seeds[4], part), 71), part)
    return dict(orbitals=orbitals, band_group=band_group, occ_table=occ_table, core_density=core_density)


solvent_eps = 78.36
density_low = 2.0
density_high = 12.0
screening = 0.05
coupling = 1.0 / (4.0 * math.pi)


def band_weights(band_group, occ_table):
    levels = occ_table.shape[0]
    matches = band_group[:, None] == jnp.arange(levels, dtype=jnp.int32)[None, :]
    chosen = jnp.where(matches, occ_table[None, :], 0)
    return jnp.sum(chosen, axis=1).astype(jnp.float32) / 1024.0


def dielectric(density):
    span = math.log(density_high) - math.log(density_low)
    fraction = jnp.clip((math.log(density_high) - jnp.log(density)) / span, 0.0, 1.0)
    turned = 2.0 * math.pi * fraction
    return jnp.exp(math.log(solvent_eps) / (2.0 * math.pi) * (turned - jnp.sin(turned)))


def reference(orbitals, band_group, occ_table, core_density):
    weights = band_weights(band_group, occ_table)

    def accumulate(running, entry):
        orbital, weight = entry
        return running + weight * jnp.square(orbital.astype(jnp.float32)), None

    electrons, _ = lax.scan(accumulate, jnp.zeros(orbitals.shape[1:], jnp.float32), (orbitals, weights))
    density = electrons + core_density
    source = electrons - core_density
    eps = dielectric(density)
    half = 0.5 * coupling
    coefs = []
    for axis in range(3):
        coefs.append(half * (eps + jnp.roll(eps, 1, axis)))
        coefs.append(half * (eps + jnp.roll(eps, -1, axis)))
    diagonal = screening + coefs[0] + coefs[1] + coefs[2] + coefs[3] + coefs[4] + coefs[5]

    def operate(values):
        result = diagonal * values
        for axis in range(3):
            result = result - coefs[2 * axis] * jnp.roll(values, 1, axis)
            result = result - coefs[2 * axis + 1] * jnp.roll(values, -1, axis)
        return result

    potential = jnp.zeros_like(source)
    residual = source
    precond = residual / diagonal
    direction = precond
    inner_now = jnp.sum(residual * precond)
    for step in range(ITERS):
        image = operate(direction)
        step_size = inner_now / jnp.sum(direction * image)
        potential = potential + step_size * direction
        residual = residual - step_size * image
        precond = residual / diagonal
        inner_next = jnp.sum(residual * precond)
        direction = precond + (inner_next / inner_now) * direction
        inner_now = inner_next
    return potential, residual
```

```python
import functools
import math

import jax
import jax.numpy as jnp
from jax import lax
from jax.experimental import pallas as pl
from jax.experimental.pallas import tpu as pltpu
from jax.sharding import PartitionSpec as P

ITERS = 3
ROWS = 32

solvent_eps = 78.36
density_low = 2.0
density_high = 12.0
screening = 0.05
coupling = 1.0 / (4.0 * math.pi)

SINE = (6.2831854820251465, -41.34170150756836, 81.6052474975586, -76.70575714111328, 42.057369232177734, -15.084554672241211, 3.7759575843811035, -0.6150599122047424)


def dielectric(density):
    span = math.log(density_high) - math.log(density_low)
    fraction = jnp.clip((math.log(density_high) - jnp.log(density)) * (1.0 / span), 0.0, 1.0)
    g = fraction - 0.5
    square = g * g
    poly = jnp.full_like(g, SINE[-1])
    for c in SINE[-2::-1]:
        poly = poly * square + c
    turned = 2.0 * math.pi * fraction
    return jnp.exp(math.log(solvent_eps) / (2.0 * math.pi) * (turned + g * poly))


def coefficients(mu, d):
    zero = jnp.zeros_like(mu[0])
    rho = [zero + 1.0]
    direction = [zero + 1.0]
    xi = [zero] * ITERS
    rz = mu[0]
    for step in range(ITERS):
        pap = zero
        for i, a in enumerate(direction):
            for j, b in enumerate(direction):
                pap = pap + a * b * d[i + j]
        alpha = rz / pap
        for i, a in enumerate(direction):
            xi[i] = xi[i] + alpha * a
        image = direction + [zero]
        for i, a in enumerate(direction):
            image[i + 1] = image[i + 1] - a
        rho = rho + [zero]
        rho = [a - alpha * b for a, b in zip(rho, image)]
        if step + 1 < ITERS:
            new = zero
            for i, a in enumerate(rho):
                for j, b in enumerate(rho):
                    new = new + a * b * mu[i + j]
            beta = new / rz
            old = direction + [zero]
            direction = [a + beta * b for a, b in zip(rho, old)]
            rz = new
    return xi, rho


def kernel(gz, orb, bg, occ, core, pot, res, obuf, cbuf, own, sent, got, eps,
           v0, v1, v2, v3, diag, coef, potbuf, resbuf, acc, red,
           in_sem, core_sem, send_sem, recv_sem, rsend, rrecv, out_sem):
    bands, nz, ny, nx = orb.shape
    half_rows = ny // 2
    chunks = half_rows // ROWS
    peers = 2 * gz
    b = lax.axis_index("band")
    z_me = lax.axis_index("gz")
    me = z_me * 2 + b
    base = pl.multiple_of(b * half_rows, half_rows)
    other = pl.multiple_of((1 - b) * half_rows, half_rows)
    partner = {"band": 1 - b}
    up = {"gz": lax.rem(z_me + 1, gz)}
    down = {"gz": lax.rem(z_me + gz - 1, gz)}
    MESH = pl.DeviceIdType.MESH

    def order(i):
        odd = i % 2
        return odd * (nz - 1 - i // 2) + (1 - odd) * (i // 2)

    def plane_in(z):
        return pltpu.make_async_copy(orb.at[:, z], obuf.at[:, z], in_sem.at[z])

    core_in = pltpu.make_async_copy(core.at[:, pl.ds(base, half_rows)], cbuf, core_sem)

    def start_in(i, _):
        plane_in(order(i)).start()
        return 0

    lax.fori_loop(0, nz, start_in, 0)
    core_in.start()

    barrier = pltpu.get_barrier_semaphore()

    def peer_id(j):
        p = lax.rem(me + j, peers)
        return {"gz": p // 2, "band": p % 2}

    def greet(j, _):
        pl.semaphore_signal(barrier, inc=1, device_id=peer_id(j), device_id_type=MESH)
        return 0

    lax.fori_loop(1, peers, greet, 0)
    acc[...] = jnp.zeros_like(acc)
    weights = [occ[bg[k]].astype(jnp.float32) * (1.0 / 1024.0) for k in range(bands)]
    pl.semaphore_wait(barrier, peers - 1)

    def remote(src, dst, s, device):
        return pltpu.make_async_remote_copy(
            src_ref=src, dst_ref=dst, send_sem=send_sem.at[s], recv_sem=recv_sem.at[s],
            device_id=device, device_id_type=MESH)

    def partial_copy(z):
        return remote(sent.at[z], got.at[z], z, partner)

    def squares(z, start, r):
        total = None
        for k in range(bands):
            value = obuf[k, z, pl.ds(start + r * ROWS, ROWS), :].astype(jnp.float32)
            term = weights[k] * (value * value)
            total = term if total is None else total + term
        return total

    def density_plane(i, _):
        z = order(i)
        plane_in(z).wait()

        def theirs(r, _):
            sent[z, pl.ds(r * ROWS, ROWS), :] = squares(z, other, r)
            return 0

        lax.fori_loop(0, chunks, theirs, 0)
        partial_copy(z).start()

        def mine(r, _):
            own[z, pl.ds(r * ROWS, ROWS), :] = squares(z, base, r)
            return 0

        lax.fori_loop(0, chunks, mine, 0)
        return 0

    lax.fori_loop(0, nz, density_plane, 0)
    core_in.wait()

    mine_rows = pl.ds(base, half_rows)

    def edges(buf, s):
        s = nz + 5 * s
        first, last = buf.at[1, mine_rows], buf.at[nz, mine_rows]
        return [
            remote(first, buf.at[nz + 1, mine_rows], s, down),
            remote(last, buf.at[0, mine_rows], s + 1, up),
            remote(first, first, s + 2, partner),
            remote(last, last, s + 3, partner),
        ]

    def inner(buf, s):
        ref = buf.at[pl.ds(2, nz - 2), mine_rows]
        return remote(ref, ref, nz + 5 * s + 4, partner)

    def eps_plane(i, _):
        z = order(i)
        partial_copy(z).wait_recv()

        def chunk(r, _):
            rows = pl.ds(r * ROWS, ROWS)
            electrons = own[z, rows, :] + got[z, rows, :]
            ion = cbuf[z, rows, :]
            own[z, rows, :] = electrons - ion
            eps[z + 1, pl.ds(base + r * ROWS, ROWS), :] = dielectric(electrons + ion)
            return 0

        lax.fori_loop(0, chunks, chunk, 0)
        return 0

    lax.fori_loop(0, 2, eps_plane, 0)
    for c in edges(eps, 0):
        c.start()
    lax.fori_loop(2, nz, eps_plane, 0)
    inner(eps, 0).start()

    row_id = lax.broadcasted_iota(jnp.int32, (ROWS, nx), 0)

    def around(buf, z, r):
        start = pl.multiple_of(base + r * ROWS, ROWS)
        center = buf[z + 1, pl.ds(start, ROWS), :]
        before = buf[z + 1, pl.ds(lax.rem(start + ny - 1, ny), 1), :]
        after = buf[z + 1, pl.ds(lax.rem(start + ROWS, ny), 1), :]
        return center, (
            buf[z, pl.ds(start, ROWS), :],
            buf[z + 2, pl.ds(start, ROWS), :],
            jnp.where(row_id == 0, before, pltpu.roll(center, 1, 0)),
            jnp.where(row_id == ROWS - 1, after, pltpu.roll(center, ROWS - 1, 0)),
            pltpu.roll(center, 1, 1),
            pltpu.roll(center, nx - 1, 1),
        )

    half = 0.5 * coupling

    def coef_chunk(z, r):
        rows = pl.ds(r * ROWS, ROWS)
        center, sides = around(eps, z, r)
        faces = [half * (center + side) for side in sides]
        d = screening + faces[0] + faces[1] + faces[2] + faces[3] + faces[4] + faces[5]
        inverse = 1.0 / d
        diag[z, rows, :] = d
        for f in range(6):
            coef[f, z, rows, :] = faces[f] * inverse
        v0[z + 1, pl.ds(base + r * ROWS, ROWS), :] = own[z, rows, :] * inverse

    def fold(x):
        total = x[0:8]
        for k in range(1, ROWS // 8):
            total = total + x[8 * k:8 * k + 8]
        return total

    def jacobi_chunk(k, src, dst, z, r):
        rows = pl.ds(r * ROWS, ROWS)
        center, sides = around(src, z, r)
        total = coef[0, z, rows, :] * sides[0]
        for f in range(1, 6):
            total = total + coef[f, z, rows, :] * sides[f]
        if k < 2:
            dst[z + 1, pl.ds(base + r * ROWS, ROWS), :] = total
        else:
            dst[z, rows, :] = total
        d = diag[z, rows, :]
        scaled = d * center
        change = d * (center - total)
        acc[2 * k] += fold(center * scaled)
        acc[5 + 2 * k] += fold(center * change)
        if k < 2:
            acc[2 * k + 1] += fold(total * scaled)
            acc[6 + 2 * k] += fold(total * change)

    def stage(s, src, dst, body):
        inner(src, s).wait_recv()

        def one(i, _):
            body(1 + i // chunks, i % chunks)
            return 0

        lax.fori_loop(0, (nz - 2) * chunks, one, 0)
        if dst is not None:
            inner(dst, s + 1).start()
        for c in edges(src, s):
            c.wait_recv()

        def two(i, _):
            body((i // chunks) * (nz - 1), i % chunks)
            return 0

        lax.fori_loop(0, 2 * chunks, two, 0)
        if dst is not None:
            for c in edges(dst, s + 1):
                c.start()

    stage(0, eps, v0, coef_chunk)
    stage(1, v0, v1, functools.partial(jacobi_chunk, 0, v0, v1))
    stage(2, v1, v2, functools.partial(jacobi_chunk, 1, v1, v2))
    stage(3, v2, None, functools.partial(jacobi_chunk, 2, v2, v3))

    row16 = lax.broadcasted_iota(jnp.int32, (16, 128), 0)
    lane16 = lax.broadcasted_iota(jnp.int32, (16, 128), 1)
    sums = jnp.zeros((16, 128), jnp.float32)
    for k in range(10):
        a = acc[k]
        line = jnp.sum(a[:, :128] + a[:, 128:] if nx == 256 else a[:, :128], axis=0, keepdims=True)
        sums = jnp.where(row16 == k, line, sums)
    lanes = jnp.sum(sums, axis=1, keepdims=True)
    red[me] = jnp.sum(jnp.where(row16 == lane16, lanes, 0.0), axis=0, keepdims=True)

    def tell(j):
        return pltpu.make_async_remote_copy(
            src_ref=red.at[me], dst_ref=red.at[me], send_sem=rsend.at[j], recv_sem=rrecv.at[me],
            device_id=peer_id(j), device_id_type=MESH)

    def hear(j):
        p = lax.rem(me + j, peers)
        return pltpu.make_async_remote_copy(
            src_ref=red.at[p], dst_ref=red.at[p], send_sem=rsend.at[j], recv_sem=rrecv.at[p],
            device_id=peer_id(j), device_id_type=MESH)

    def start_tell(j, _):
        tell(j).start()
        return 0

    lax.fori_loop(1, peers, start_tell, 0)

    def wait_hear(j, _):
        hear(j).wait_recv()
        return 0

    lax.fori_loop(1, peers, wait_hear, 0)

    line = jnp.sum(red[...], axis=0)
    totals = jnp.sum(jnp.where(row16 == lane16, line, 0.0), axis=1, keepdims=True)
    wide = jnp.broadcast_to(totals, (16, nx))
    xi, rho = coefficients([wide[k:k + 1] for k in range(5)], [wide[5 + k:6 + k] for k in range(5)])

    def out_copies(z):
        return (
            pltpu.make_async_copy(potbuf.at[z], pot.at[z], out_sem.at[z]),
            pltpu.make_async_copy(resbuf.at[z], res.at[z], out_sem.at[nz + z]),
        )

    def finish(z, _):
        def mine(r, _):
            rows = pl.ds(r * ROWS, ROWS)
            at = pl.ds(base + r * ROWS, ROWS)
            a, c, e = v0[z + 1, at, :], v1[z + 1, at, :], v2[z + 1, at, :]
            potbuf[z, at, :] = xi[0] * a + xi[1] * c + xi[2] * e
            resbuf[z, rows, :] = diag[z, rows, :] * (
                rho[0] * a + rho[1] * c + rho[2] * e + rho[3] * v3[z, rows, :])
            return 0

        def theirs(r, _):
            at = pl.ds(other + r * ROWS, ROWS)
            potbuf[z, at, :] = xi[0] * v0[z + 1, at, :] + xi[1] * v1[z + 1, at, :] + xi[2] * v2[z + 1, at, :]
            return 0

        lax.fori_loop(0, chunks, mine, 0)
        lax.fori_loop(0, chunks, theirs, 0)
        for c in out_copies(z):
            c.start()
        return 0

    lax.fori_loop(0, nz, finish, 0)

    def drain(z, _):
        partial_copy(z).wait_send()
        for c in out_copies(z):
            c.wait()
        return 0

    lax.fori_loop(0, nz, drain, 0)
    for s, buf in enumerate((eps, v0, v1, v2)):
        for c in edges(buf, s):
            c.wait_send()
        inner(buf, s).wait_send()

    def told(j, _):
        tell(j).wait_send()
        return 0

    lax.fori_loop(1, peers, told, 0)


def per_device(gz, orbitals, band_group, occ_table, core_density):
    bands, nz, ny, nx = orbitals.shape
    h = ny // 2
    f32 = jnp.float32
    full = pltpu.VMEM((nz + 2, ny, nx), f32)
    tile = pltpu.VMEM((nz, h, nx), f32)
    copies = nz + 20
    return pl.pallas_call(
        functools.partial(kernel, gz),
        out_shape=(
            jax.ShapeDtypeStruct((nz, ny, nx), f32),
            jax.ShapeDtypeStruct((nz, h, nx), f32),
        ),
        in_specs=[
            pl.BlockSpec(memory_space=pl.ANY),
            pl.BlockSpec(memory_space=pltpu.SMEM),
            pl.BlockSpec(memory_space=pltpu.SMEM),
            pl.BlockSpec(memory_space=pl.ANY),
        ],
        out_specs=(pl.BlockSpec(memory_space=pl.ANY), pl.BlockSpec(memory_space=pl.ANY)),
        scratch_shapes=[
            pltpu.VMEM((bands, nz, ny, nx), jnp.bfloat16),
            tile, tile, tile, tile,
            full, full, full, full,
            tile, tile,
            pltpu.VMEM((6, nz, h, nx), f32),
            pltpu.VMEM((nz, ny, nx), f32),
            tile,
            pltpu.VMEM((10, 8, nx), f32),
            pltpu.VMEM((2 * gz, 1, 128), f32),
            pltpu.SemaphoreType.DMA((nz,)),
            pltpu.SemaphoreType.DMA,
            pltpu.SemaphoreType.DMA((copies,)),
            pltpu.SemaphoreType.DMA((copies,)),
            pltpu.SemaphoreType.DMA((2 * gz,)),
            pltpu.SemaphoreType.DMA((2 * gz,)),
            pltpu.SemaphoreType.DMA((2 * nz,)),
        ],
        compiler_params=pltpu.CompilerParams(
            collective_id=0, has_side_effects=True, vmem_limit_bytes=50 * 1024 * 1024
        ),
        cost_estimate=pl.CostEstimate(flops=30000000, bytes_accessed=12000000, transcendentals=1000000),
        name="poisson",
    )(orbitals, band_group, occ_table, core_density)


def solution(mesh):
    assert mesh.shape["band"] == 2
    return jax.shard_map(
        functools.partial(per_device, mesh.shape["gz"]),
        mesh=mesh,
        in_specs=(
            P(("groups", "band"), "gz", None, None),
            P(("groups", "band")),
            P(),
            P(("groups", "gz"), None, None),
        ),
        out_specs=(P(("groups", "gz"), None, None), P(("groups", "gz"), "band", None)),
        check_vma=False,
    )
```

```python
import functools
import math

import jax
import jax.numpy as jnp
from jax import lax
from jax.experimental import pallas as pl
from jax.experimental.pallas import tpu as pltpu
from jax.sharding import PartitionSpec as P

ITERS = 3
ROWS = 32

solvent_eps = 78.36
density_low = 2.0
density_high = 12.0
screening = 0.05
coupling = 1.0 / (4.0 * math.pi)

SINE = (6.2831854820251465, -41.34170150756836, 81.6052474975586, -76.70575714111328, 42.057369232177734, -15.084554672241211, 3.7759575843811035, -0.6150599122047424)


def dielectric(density):
    span = math.log(density_high) - math.log(density_low)
    fraction = jnp.clip((math.log(density_high) - jnp.log(density)) * (1.0 / span), 0.0, 1.0)
    g = fraction - 0.5
    square = g * g
    poly = jnp.full_like(g, SINE[-1])
    for c in SINE[-2::-1]:
        poly = poly * square + c
    turned = 2.0 * math.pi * fraction
    return jnp.exp(math.log(solvent_eps) / (2.0 * math.pi) * (turned + g * poly))


def coefficients(mu, d):
    zero = jnp.zeros_like(mu[0])
    rho = [zero + 1.0]
    direction = [zero + 1.0]
    xi = [zero] * ITERS
    rz = mu[0]
    for step in range(ITERS):
        pap = zero
        for i, a in enumerate(direction):
            for j, b in enumerate(direction):
                pap = pap + a * b * d[i + j]
        alpha = rz / pap
        for i, a in enumerate(direction):
            xi[i] = xi[i] + alpha * a
        image = direction + [zero]
        for i, a in enumerate(direction):
            image[i + 1] = image[i + 1] - a
        rho = rho + [zero]
        rho = [a - alpha * b for a, b in zip(rho, image)]
        if step + 1 < ITERS:
            new = zero
            for i, a in enumerate(rho):
                for j, b in enumerate(rho):
                    new = new + a * b * mu[i + j]
            beta = new / rz
            old = direction + [zero]
            direction = [a + beta * b for a, b in zip(rho, old)]
            rz = new
    return xi, rho


def kernel(gz, orb, bg_in, occ_in, core, pot, res, obuf, cbuf, own, sent, got, eps,
           v0, v1, v2, v3, diag, coef, potbuf, resbuf, ys, yh, acc, red,
           bg, occ, small_sem, in_sem, core_sem, send_sem, recv_sem, rsend, rrecv, out_sem):
    bands, nz, ny, nx = orb.shape
    half_rows = ny // 2
    chunks = half_rows // ROWS
    peers = 2 * gz
    b = lax.axis_index("band")
    z_me = lax.axis_index("gz")
    me = z_me * 2 + b
    base = pl.multiple_of(b * half_rows, half_rows)
    other = pl.multiple_of((1 - b) * half_rows, half_rows)
    partner = {"band": 1 - b}
    up = {"gz": lax.rem(z_me + 1, gz)}
    down = {"gz": lax.rem(z_me + gz - 1, gz)}
    MESH = pl.DeviceIdType.MESH

    def order(i):
        odd = i % 2
        return odd * (nz - 1 - i // 2) + (1 - odd) * (i // 2)

    def plane_in(z):
        return pltpu.make_async_copy(orb.at[:, z], obuf.at[:, z], in_sem.at[z])

    core_in = pltpu.make_async_copy(core.at[:, pl.ds(base, half_rows)], cbuf, core_sem)

    def start_in(i, _):
        plane_in(order(i)).start()
        return 0

    small_in = (
        pltpu.make_async_copy(bg_in, bg, small_sem.at[0]),
        pltpu.make_async_copy(occ_in, occ, small_sem.at[1]),
    )
    for c in small_in:
        c.start()
    lax.fori_loop(0, nz, start_in, 0)
    core_in.start()

    barrier = pltpu.get_barrier_semaphore()

    def peer_id(j):
        p = lax.rem(me + j, peers)
        return {"gz": p // 2, "band": p % 2}

    def greet(j, _):
        pl.semaphore_signal(barrier, inc=1, device_id=peer_id(j), device_id_type=MESH)
        return 0

    lax.fori_loop(1, peers, greet, 0)
    acc[...] = jnp.zeros_like(acc)
    for c in small_in:
        c.wait()
    weights = [occ[bg[k]].astype(jnp.float32) * (1.0 / 1024.0) for k in range(bands)]
    pl.semaphore_wait(barrier, peers - 1)

    def remote(src, dst, s, device):
        return pltpu.make_async_remote_copy(
            src_ref=src, dst_ref=dst, send_sem=send_sem.at[s], recv_sem=recv_sem.at[s],
            device_id=device, device_id_type=MESH)

    def partial_copy(z):
        return remote(sent.at[z], got.at[z], z, partner)

    def squares(z, start, r):
        total = None
        for k in range(bands):
            value = obuf[k, z, pl.ds(start + r * ROWS, ROWS), :].astype(jnp.float32)
            term = weights[k] * (value * value)
            total = term if total is None else total + term
        return total

    def density_plane(i, _):
        z = order(i)
        plane_in(z).wait()

        def theirs(r, _):
            sent[z, pl.ds(r * ROWS, ROWS), :] = squares(z, other, r)
            return 0

        lax.fori_loop(0, chunks, theirs, 0, unroll=4)
        partial_copy(z).start()

        def mine(r, _):
            own[z, pl.ds(r * ROWS, ROWS), :] = squares(z, base, r)
            return 0

        lax.fori_loop(0, chunks, mine, 0, unroll=4)
        return 0

    lax.fori_loop(0, nz, density_plane, 0)
    core_in.wait()

    mine_rows = pl.ds(base, half_rows)

    def edges(buf, k):
        s = nz + 5 * k
        first, last = buf.at[1, mine_rows], buf.at[nz, mine_rows]
        return [
            remote(first, buf.at[nz + 1, mine_rows], s, down),
            remote(last, buf.at[0, mine_rows], s + 1, up),
            remote(ys.at[k, pl.ds(0, 2)], yh.at[k, pl.ds(0, 2)], s + 2, partner),
            remote(ys.at[k, pl.ds(2 * nz - 2, 2)], yh.at[k, pl.ds(2 * nz - 2, 2)], s + 3, partner),
        ]

    def inner(s):
        rows = pl.ds(2, 2 * nz - 4)
        return remote(ys.at[s, rows], yh.at[s, rows], nz + 5 * s + 4, partner)

    def answer(z):
        ref = potbuf.at[z, mine_rows]
        return remote(ref, ref, nz + 20 + z, partner)

    def keep_rows(s, z, r, value):
        if r == 0:
            ys[s, 2 * z] = value[:1]
        if r == chunks - 1:
            ys[s, 2 * z + 1] = value[ROWS - 1:]

    def eps_plane(i, _):
        z = order(i)
        partial_copy(z).wait_recv()

        def chunk(r, _):
            rows = pl.ds(r * ROWS, ROWS)
            electrons = own[z, rows, :] + got[z, rows, :]
            ion = cbuf[z, rows, :]
            own[z, rows, :] = electrons - ion
            value = dielectric(electrons + ion)
            eps[z + 1, pl.ds(base + r * ROWS, ROWS), :] = value
            keep_rows(0, z, r, value)

        for r in range(chunks):
            chunk(r, 0)
        return 0

    lax.fori_loop(0, 2, eps_plane, 0)
    for c in edges(eps, 0):
        c.start()
    lax.fori_loop(2, nz, eps_plane, 0)
    inner(0).start()

    row_id = lax.broadcasted_iota(jnp.int32, (ROWS, nx), 0)

    def around(buf, s, z, r):
        start = pl.multiple_of(base + r * ROWS, ROWS)
        center = buf[z + 1, pl.ds(start, ROWS), :]
        before = buf[z + 1, pl.ds(start - 1, 1), :] if r > 0 else yh[s, 2 * z + 1]
        after = buf[z + 1, pl.ds(start + ROWS, 1), :] if r < chunks - 1 else yh[s, 2 * z]
        return center, (
            buf[z, pl.ds(start, ROWS), :],
            buf[z + 2, pl.ds(start, ROWS), :],
            jnp.where(row_id == 0, before, pltpu.roll(center, 1, 0)),
            jnp.where(row_id == ROWS - 1, after, pltpu.roll(center, ROWS - 1, 0)),
            pltpu.roll(center, 1, 1),
            pltpu.roll(center, nx - 1, 1),
        )

    half = 0.5 * coupling

    def coef_chunk(z, r):
        rows = pl.ds(r * ROWS, ROWS)
        center, sides = around(eps, 0, z, r)
        faces = [half * (center + side) for side in sides]
        d = screening + faces[0] + faces[1] + faces[2] + faces[3] + faces[4] + faces[5]
        inverse = 1.0 / d
        diag[z, rows, :] = d
        for f in range(6):
            coef[f, z, rows, :] = faces[f] * inverse
        value = own[z, rows, :] * inverse
        v0[z + 1, pl.ds(base + r * ROWS, ROWS), :] = value
        keep_rows(1, z, r, value)

    def fold(x):
        total = x[0:8]
        for k in range(1, ROWS // 8):
            total = total + x[8 * k:8 * k + 8]
        return total

    def jacobi_chunk(k, src, dst, z, r):
        rows = pl.ds(r * ROWS, ROWS)
        center, sides = around(src, k + 1, z, r)
        total = coef[0, z, rows, :] * sides[0]
        for f in range(1, 6):
            total = total + coef[f, z, rows, :] * sides[f]
        if k < 2:
            dst[z + 1, pl.ds(base + r * ROWS, ROWS), :] = total
            keep_rows(k + 2, z, r, total)
        else:
            dst[z, rows, :] = total
        d = diag[z, rows, :]
        scaled = d * center
        change = d * (center - total)
        sums = [fold(center * scaled), fold(center * change)]
        if k < 2:
            sums += [fold(total * scaled), fold(total * change)]
        return sums

    def stage(s, src, dst, body):
        k0 = 4 * (s - 1)
        inner(s).wait_recv()

        def plane(z):
            sums = [body(z, r) for r in range(chunks)]
            if sums[0] is not None:
                for k, parts in enumerate(zip(*sums)):
                    acc[k0 + k] += sum(parts[1:], parts[0])

        def one(z, _):
            plane(z)
            return 0

        lax.fori_loop(1, nz - 1, one, 0)
        if dst is not None:
            inner(s + 1).start()
        for c in edges(src, s):
            c.wait_recv()

        def two(i, _):
            plane(i * (nz - 1))
            return 0

        lax.fori_loop(0, 2, two, 0)
        if dst is not None:
            for c in edges(dst, s + 1):
                c.start()

    stage(0, eps, v0, coef_chunk)
    stage(1, v0, v1, functools.partial(jacobi_chunk, 0, v0, v1))
    stage(2, v1, v2, functools.partial(jacobi_chunk, 1, v1, v2))
    stage(3, v2, None, functools.partial(jacobi_chunk, 2, v2, v3))

    row16 = lax.broadcasted_iota(jnp.int32, (16, 128), 0)
    lane16 = lax.broadcasted_iota(jnp.int32, (16, 128), 1)
    sums = jnp.zeros((16, 128), jnp.float32)
    for k in range(10):
        a = acc[k]
        line = jnp.sum(a[:, :128] + a[:, 128:] if nx == 256 else a[:, :128], axis=0, keepdims=True)
        sums = jnp.where(row16 == k, line, sums)
    lanes = jnp.sum(sums, axis=1, keepdims=True)
    red[me] = jnp.sum(jnp.where(row16 == lane16, lanes, 0.0), axis=0, keepdims=True)

    def tell(j):
        return pltpu.make_async_remote_copy(
            src_ref=red.at[me], dst_ref=red.at[me], send_sem=rsend.at[j], recv_sem=rrecv.at[me],
            device_id=peer_id(j), device_id_type=MESH)

    def hear(j):
        p = lax.rem(me + j, peers)
        return pltpu.make_async_remote_copy(
            src_ref=red.at[p], dst_ref=red.at[p], send_sem=rsend.at[j], recv_sem=rrecv.at[p],
            device_id=peer_id(j), device_id_type=MESH)

    def start_tell(j, _):
        tell(j).start()
        return 0

    lax.fori_loop(1, peers, start_tell, 0)

    def wait_hear(j, _):
        hear(j).wait_recv()
        return 0

    lax.fori_loop(1, peers, wait_hear, 0)

    line = jnp.sum(red[...], axis=0)
    totals = jnp.sum(jnp.where(row16 == lane16, line, 0.0), axis=1, keepdims=True)
    wide = jnp.broadcast_to(totals, (16, nx))
    xi, rho = coefficients([wide[k:k + 1] for k in range(0, 10, 2)], [wide[k:k + 1] for k in range(1, 10, 2)])

    def out_copies(z):
        return (
            pltpu.make_async_copy(potbuf.at[z], pot.at[z], out_sem.at[z]),
            pltpu.make_async_copy(resbuf.at[z], res.at[z], out_sem.at[nz + z]),
        )

    def potential_plane(z, _):
        for r in range(chunks):
            at = pl.ds(base + r * ROWS, ROWS)
            potbuf[z, at, :] = xi[0] * v0[z + 1, at, :] + xi[1] * v1[z + 1, at, :] + xi[2] * v2[z + 1, at, :]
        answer(z).start()
        return 0

    def residual_plane(z, _):
        for r in range(chunks):
            rows = pl.ds(r * ROWS, ROWS)
            at = pl.ds(base + r * ROWS, ROWS)
            resbuf[z, rows, :] = diag[z, rows, :] * (
                rho[0] * v0[z + 1, at, :] + rho[1] * v1[z + 1, at, :]
                + rho[2] * v2[z + 1, at, :] + rho[3] * v3[z, rows, :])
        out_copies(z)[1].start()
        return 0

    def potential_out(z, _):
        answer(z).wait_recv()
        out_copies(z)[0].start()
        return 0

    lax.fori_loop(0, nz, potential_plane, 0)
    lax.fori_loop(0, nz, residual_plane, 0)
    lax.fori_loop(0, nz, potential_out, 0)

    def drain(z, _):
        partial_copy(z).wait_send()
        answer(z).wait_send()
        for c in out_copies(z):
            c.wait()
        return 0

    lax.fori_loop(0, nz, drain, 0)
    for s, buf in enumerate((eps, v0, v1, v2)):
        for c in edges(buf, s):
            c.wait_send()
        inner(s).wait_send()

    def told(j, _):
        tell(j).wait_send()
        return 0

    lax.fori_loop(1, peers, told, 0)


def per_device(gz, orbitals, band_group, occ_table, core_density):
    bands, nz, ny, nx = orbitals.shape
    h = ny // 2
    f32 = jnp.float32
    full = pltpu.VMEM((nz + 2, ny, nx), f32)
    tile = pltpu.VMEM((nz, h, nx), f32)
    copies = 2 * nz + 20
    return pl.pallas_call(
        functools.partial(kernel, gz),
        out_shape=(
            jax.ShapeDtypeStruct((nz, ny, nx), f32),
            jax.ShapeDtypeStruct((nz, h, nx), f32),
        ),
        in_specs=[
            pl.BlockSpec(memory_space=pltpu.HBM),
            pl.BlockSpec(memory_space=pltpu.HBM),
            pl.BlockSpec(memory_space=pltpu.HBM),
            pl.BlockSpec(memory_space=pltpu.HBM),
        ],
        out_specs=(pl.BlockSpec(memory_space=pl.ANY), pl.BlockSpec(memory_space=pl.ANY)),
        scratch_shapes=[
            pltpu.VMEM((bands, nz, ny, nx), jnp.bfloat16),
            tile, tile, tile, tile,
            full, full, full, full,
            tile, tile,
            pltpu.VMEM((6, nz, h, nx), f32),
            pltpu.VMEM((nz, ny, nx), f32),
            tile,
            pltpu.VMEM((4, 2 * nz, 1, nx), f32),
            pltpu.VMEM((4, 2 * nz, 1, nx), f32),
            pltpu.VMEM((10, 8, nx), f32),
            pltpu.VMEM((2 * gz, 1, 128), f32),
            pltpu.SMEM(band_group.shape, jnp.int32),
            pltpu.SMEM(occ_table.shape, jnp.int32),
            pltpu.SemaphoreType.DMA((2,)),
            pltpu.SemaphoreType.DMA((nz,)),
            pltpu.SemaphoreType.DMA,
            pltpu.SemaphoreType.DMA((copies,)),
            pltpu.SemaphoreType.DMA((copies,)),
            pltpu.SemaphoreType.DMA((2 * gz,)),
            pltpu.SemaphoreType.DMA((2 * gz,)),
            pltpu.SemaphoreType.DMA((2 * nz,)),
        ],
        compiler_params=pltpu.CompilerParams(
            collective_id=0, has_side_effects=True, vmem_limit_bytes=50 * 1024 * 1024
        ),
        cost_estimate=pl.CostEstimate(flops=30000000, bytes_accessed=12000000, transcendentals=1000000),
        name="poisson",
    )(orbitals, band_group, occ_table, core_density)


def solution(mesh):
    assert mesh.shape["band"] == 2
    return jax.shard_map(
        functools.partial(per_device, mesh.shape["gz"]),
        mesh=mesh,
        in_specs=(
            P(("groups", "band"), "gz", None, None),
            P(("groups", "band")),
            P(),
            P(("groups", "gz"), None, None),
        ),
        out_specs=(P(("groups", "gz"), None, None), P(("groups", "gz"), "band", None)),
        check_vma=False,
    )
```
